32 devices in a mesh: gx: 4 (over x, core), gy: 4 (over z), gz: 2 (over y).
Axes of the slice: x: 2, y: 2, z: 4, core: 2. Of those that a mesh axis runs over, the one named last changes fastest.
Arguments:
- fine_rhs: bfloat16 [96, 96, 48, 256], P('gx', 'gy', 'gz'), may hold values from -6 to 6
- coef_table: bfloat16 [256], replicated, may hold values from 0.29882812 to 3
- coef_ids: int32 [128, 512], P(('gx', 'gy', 'gz')), may hold values from 0 to 255
- localization: int32 [128, 512], P(('gx', 'gy', 'gz')), may hold values from 0 to 32767, as said below
- patch_mask: int32 [128, 512], P(('gx', 'gy', 'gz')), may hold values from 0 to 1, as said below
- measure_weights: bfloat16 [128, 512], P(('gx', 'gy', 'gz')), may hold values from 0.5 to 2
- owners: int32 [128], P(('gx', 'gy', 'gz')), may hold values from 0 to 1, as said below
Outputs:
- coarse_stiffness: float32 [128, 4096], P(('gx', 'gy', 'gz'))
- coarse_rhs: float32 [128, 16384], P(('gx', 'gy', 'gz'))
The draws below stay inside these ranges and needn't reach their ends.
Inputs may be any that keep to these rules, and one draw needn't show every extreme that they name: `localization`: each patch's list is a box of 8 x 8 x 8 consecutive cells of the device's block extended by 4 cells on every side (extent 24 + 2 * 4), in row-major order with the first dimension slowest; on every device the first patch's box starts at the extended block's first cell and the second's ends at its last. `patch_mask`: in every 2 x 2 x 2 subcell of a patch's box the dof whose three box coordinates are all even is live. `owners`: no device names one owner for more than 2 of its patches; in each group of devices that differ only in the gz index, one owner gets exactly 2 patches from every device of the group.
All inputs are finite; a program needn't handle non-finite values.
Results may differ from the reference program's by a relative error of at most 0.0003.
Values may be sent and summed in bfloat16 or wider, within the bound.
A program may use at most 128 MiB of HBM per device.

```python
import math
import jax
import jax.numpy as jnp
from jax import lax

C = 24
RHS = 256
BOX = 8
HW = 4
NP = 4
NCOEF = 256
PATCH = 512
M = 64
NX = 96
NY = 96
NZ = 48
PATCHES = 128
SLOTS = 128
N_GY = 4
N_GZ = 2


def box_positions():
    dof_index = jnp.arange(PATCH, dtype=jnp.int32)
    return (dof_index // (BOX * BOX), dof_index // BOX % BOX, dof_index % BOX)


def draw_localization(key, part):
    extent = C + 2 * HW
    corner_room = extent - BOX + 1
    corner = jax.random.randint(key, (PATCHES, 3), 0, corner_room)
    slot_rank = jnp.arange(PATCHES, dtype=jnp.int32) % NP
    corner = jnp.where((slot_rank == 0)[:, None], 0, corner)
    corner = jnp.where((slot_rank == 1)[:, None], corner_room - 1, corner)
    along_one, along_two, along_three = box_positions()
    cells = ((corner[:, 0:1] + along_one[None, :]) * extent + corner[:, 1:2] + along_two[None, :]) * extent
    cells = cells + corner[:, 2:3] + along_three[None, :]
    return cells.astype(jnp.int32)


def draw_patch_mask(key, part):
    coin_flip = jax.random.randint(key, (PATCHES, PATCH), 0, 4)
    along_one, along_two, along_three = box_positions()
    anchor = (along_one % 2 == 0) & (along_two % 2 == 0) & (along_three % 2 == 0)
    return jnp.where(anchor[None, :] | (coin_flip > 0), 1, 0).astype(jnp.int32)


def draw_owners(key, part):
    devices = PATCHES // NP
    groups = devices // N_GZ
    capacity = max(NP // 4, (NP + N_GZ - 1) // N_GZ)
    target = jax.random.randint(jax.random.fold_in(key, 1), (groups,), 0, N_GZ)
    scores = jax.random.randint(jax.random.fold_in(key, 2), (devices, NP), 0, 1 << 20) * NP
    scores = scores + jnp.arange(NP, dtype=jnp.int32)[None, :]
    ordering = jnp.argsort(scores, axis=1)
    position = jnp.argsort(ordering, axis=1).astype(jnp.int32)
    rotation = jax.random.randint(jax.random.fold_in(key, 3), (devices, 1), 0, N_GZ - 1)
    target_each = jnp.repeat(target, N_GZ)[:, None]
    other = (target_each + 1 + (position - capacity + rotation) % (N_GZ - 1)) % N_GZ
    owner_map = jnp.where(position < capacity, target_each, other)
    return owner_map.reshape(PATCHES).astype(jnp.int32)


def set_ends(result, rng, smallest, high):
    shape = result.shape
    spot = [jax.random.randint(jax.random.fold_in(rng, axis), (), 0, shape[axis]) for axis in range(len(shape))]
    result = result.at[tuple(spot)].set(smallest)
    longest = shape.index(max(shape))
    spot[longest] = (spot[longest] + 1) % shape[longest]
    return result.at[tuple(spot)].set(high)


def steps_of(own_key, shape, shards, smallest, high):
    level = 1.0
    for dim, shards_of in shards:
        heights = jax.random.uniform(jax.random.fold_in(jax.random.fold_in(own_key, 6), dim), (shards_of,), jnp.float32, smallest / len(shards), high / len(shards))
        level = level * jnp.repeat(jnp.exp(heights), shape[dim] // shards_of).reshape((-1,) + (1,) * (len(shape) - 1 - dim))
    return level


def gaussian(own_key, shape, spread, limit, shards=(), kind=jnp.bfloat16):
    drawn = spread * jax.random.normal(own_key, shape, jnp.float32)
    if shards:
        drawn = drawn * steps_of(own_key, shape, shards, -0.22, 0.18)
    return jnp.clip(drawn, -limit, limit).astype(kind)


def setup_inputs(seed: int = 0) -> dict:
    splits = jax.random.split(jax.random.key(seed), 8)
    fine_rhs = gaussian(splits[0], (NX, NY, NZ, RHS), 1.0, 6.0, ((0, 4), (1, 4), (2, 2)))
    coef_table = jnp.clip(jnp.exp(jax.random.uniform(splits[1], (NCOEF,), jnp.float32, math.log(0.29882812), math.log(3.0))), 0.29882812, 3.0).astype(jnp.bfloat16)
    coef_ids = set_ends(jax.random.randint(splits[2], (PATCHES, PATCH), 0, NCOEF), jax.random.fold_in(splits[2], 1), 0, NCOEF - 1).astype(jnp.int32)
    localization = draw_localization(jax.random.fold_in(splits[7], 71), 0)
    patch_mask = draw_patch_mask(jax.random.fold_in(splits[7], 71), 0)
    measure_weights = jnp.clip(jnp.exp(math.log(2.0) - 1.3862944 * jax.random.uniform(splits[5], (PATCHES, PATCH), jnp.float32) ** steps_of(splits[5], (PATCHES, PATCH), ((0, 32),), -0.2, 0.2)), 0.5, 2.0).astype(jnp.bfloat16)
    owners = draw_owners(jax.random.fold_in(splits[7], 71), 0)
    return {"fine_rhs": fine_rhs, "coef_table": coef_table, "coef_ids": coef_ids, "localization": localization, "patch_mask": patch_mask, "measure_weights": measure_weights, "owners": owners}


diag_shift = 6.5
highest = lax.Precision.HIGHEST

def box_tables():
    dof_index = jnp.arange(PATCH, dtype=jnp.int32)
    along_one = dof_index // (BOX * BOX)
    along_two = dof_index // BOX % BOX
    along_three = dof_index % BOX
    distance = jnp.abs(along_one[:, None] - along_one[None, :]) + jnp.abs(along_two[:, None] - along_two[None, :]) + jnp.abs(along_three[:, None] - along_three[None, :])
    adjacency = jnp.where(distance == 1, 1.0, 0.0).astype(jnp.float32)
    half_box = BOX // 2
    subcell = (along_one // 2 * half_box + along_two // 2) * half_box + along_three // 2
    member = jnp.where(subcell[None, :] == jnp.arange(M, dtype=jnp.int32)[:, None], 1.0, 0.0).astype(jnp.float32)
    return (adjacency, member)

def solve_patch(patch_rows, coefficient, live_mask, weights, adjacency, member):
    root_coef = jnp.sqrt(coefficient)
    coupled = live_mask[:, None] * live_mask[None, :] * (diag_shift * jnp.diag(coefficient) - root_coef[:, None] * root_coef[None, :] * adjacency)
    operator = coupled + jnp.diag(1.0 - live_mask)
    measure = member * (weights * live_mask)[None, :]
    factor = jnp.linalg.cholesky(operator)
    response = jax.scipy.linalg.cho_solve((factor, True), measure.T)
    schur = jnp.dot(measure, response, precision=highest)
    occupied = jnp.max(live_mask)
    identity = jnp.eye(measure.shape[0], dtype=jnp.float32)
    schur = schur + (1.0 - occupied) * identity
    small_factor = jnp.linalg.cholesky(schur)
    coarse_block = jax.scipy.linalg.cho_solve((small_factor, True), identity) * occupied
    projected = jnp.dot(response.T, patch_rows.astype(jnp.float32), precision=highest)
    coarse_part = jnp.dot(coarse_block, projected, precision=highest)
    return (coarse_block.reshape(-1), coarse_part.reshape(-1))

def reference(fine_rhs, coef_table, coef_ids, localization, patch_mask, measure_weights, owners):
    adjacency, member = box_tables()
    extent = C + 2 * HW
    capacity = max(NP // 4, (NP + N_GZ - 1) // N_GZ)
    padded = jnp.pad(fine_rhs, ((HW, HW), (HW, HW), (HW, HW), (0, 0)))
    device = jnp.arange(PATCHES, dtype=jnp.int32) // NP
    dev_first = device // (N_GY * N_GZ)
    dev_second = device // N_GZ % N_GY
    dev_third = device % N_GZ

    def one_patch(which):
        cells = localization[which]
        cell_one = cells // (extent * extent)
        cell_two = cells // extent % extent
        cell_three = cells % extent
        patch_rows = padded[dev_first[which] * C + cell_one, dev_second[which] * C + cell_two, dev_third[which] * C + cell_three]
        coefficient = coef_table[coef_ids[which]].astype(jnp.float32)
        live_mask = patch_mask[which].astype(jnp.float32)
        weights = measure_weights[which].astype(jnp.float32)
        return solve_patch(patch_rows, coefficient, live_mask, weights, adjacency, member)
    blocks, rhs_parts = lax.map(one_patch, jnp.arange(PATCHES, dtype=jnp.int32))
    owner_blocks = owners.reshape(PATCHES // NP, NP)
    owner_hits = (owner_blocks[:, :, None] == jnp.arange(N_GZ, dtype=jnp.int32)[None, None, :]).astype(jnp.int32)
    earlier_hits = jnp.cumsum(owner_hits, axis=1) - owner_hits
    slot_rank = lax.optimization_barrier(jnp.sum(earlier_hits * owner_hits, axis=2)).reshape(PATCHES)
    destination = device - dev_third + owners
    position = (destination * (N_GZ * capacity) + dev_third * capacity + slot_rank).astype(jnp.int32)
    coarse_stiffness = jnp.zeros((SLOTS, M * M), jnp.float32).at[position].set(blocks)
    coarse_rhs = jnp.zeros((SLOTS, M * RHS), jnp.float32).at[position].set(rhs_parts)
    return (coarse_stiffness, coarse_rhs)
```

```python
import math
import jax
import jax.numpy as jnp
from jax import lax
from jax.experimental import pallas as pl
from jax.experimental.pallas import tpu as pltpu
from jax.sharding import PartitionSpec as P

BOX = 8
HW = 4
PATCH = 512
M = 64
HALF = BOX // 2

diag_shift = 6.5
radius = 6.0 * math.cos(math.pi / 9.0) / diag_shift
low, high = (1.0 - radius) * diag_shift, (1.0 + radius) * diag_shift
half_steps = 30
newton_steps = 4
highest = lax.Precision.HIGHEST


def relaxation():
    weights = [1.0, 2.0 / (2.0 - radius * radius)]
    while len(weights) < half_steps:
        weights.append(1.0 / (1.0 - radius * radius * weights[-1] / 4.0))
    return weights


def start_polynomial():
    a, b = 1.0 / high, 1.0 / low
    mid, half = (a + b) / 2.0, (b - a) / 2.0
    t = -mid / half
    top = 4.0 * t**3 - 3.0 * t
    c3 = 4.0 / half**3 / top
    c2 = -12.0 * mid / half**3 / top
    c1 = (12.0 * mid * mid / half**3 - 3.0 / half) / top
    return (-c1, -c2, -c3)


def exact_dot(a, b):
    return jnp.dot(a, b, precision=highest, preferred_element_type=jnp.float32)


def relax(new, old, bias, gate, weight, flip, place):
    for x in range(BOX):
        here = old[x]
        up = pltpu.roll(here, 1, 1)
        down = pltpu.roll(here, BOX - 1, 1)
        total = jnp.where(place == 0, 0.0, up) + jnp.where(place == BOX - 1, 0.0, down)
        zero = jnp.zeros_like(here[:1])
        before = jnp.concatenate([zero, here[:-1]], axis=0)
        after = jnp.concatenate([here[1:], zero], axis=0)
        odd = (place + (x + flip)) % 2
        total = total + here + jnp.where(odd == 0, before, after)
        if x > 0:
            total = total + old[x - 1]
        if x < BOX - 1:
            total = total + old[x + 1]
        current = new[x]
        new[x] = current + weight * (gate[x] * total + bias[x] - current)


def patch_kernel(slot_ref, omega_ref, dofs_ref, rows_ref, block_ref, part_ref,
                 red, black, bias_r, bias_k, gate_r, gate_k, root_r, root_k):
    patches = rows_ref.shape[0]
    lanes = patches * M
    spot = jnp.where(
        lax.broadcasted_iota(jnp.int32, (patches, lanes), 1) // M
        == lax.broadcasted_iota(jnp.int32, (patches, lanes), 0), 1.0, 0.0).astype(jnp.bfloat16)
    shape = (HALF, BOX, lanes)
    place = lax.broadcasted_iota(jnp.int32, shape, 1)
    column = lax.broadcasted_iota(jnp.int32, shape, 2) % M
    along = lax.broadcasted_iota(jnp.int32, shape, 0)
    for color, (bias, gate, root) in enumerate(((bias_r, gate_r, root_r), (bias_k, gate_k, root_k))):
        wide = [
            jnp.dot(dofs_ref[color, kind], spot, preferred_element_type=jnp.float32).reshape(
                (BOX, HALF, BOX, lanes))
            for kind in range(3)
        ]
        for x in range(BOX):
            live = wide[1][x]
            scale = live * lax.rsqrt(wide[0][x])
            member = (x // 2 * HALF + along) * HALF + place // 2 == column
            root[x] = scale
            gate[x] = live * (1.0 / diag_shift)
            bias[x] = jnp.where(member, scale * wide[2][x] * (1.0 / diag_shift), 0.0)
    red[...] = bias_r[...]
    black[...] = jnp.zeros(black.shape, jnp.float32)
    relax(black, red, bias_k, gate_k, omega_ref[1], 1, place)

    @pl.loop(1, half_steps // 2)
    def _(step):
        relax(red, black, bias_r, gate_r, omega_ref[2 * step], 0, place)
        relax(black, red, bias_k, gate_k, omega_ref[2 * step + 1], 1, place)

    pooled, norms, response = [], [], []
    for x2 in range(BOX // 2):
        solved, size = 0.0, 0.0
        for x in (2 * x2, 2 * x2 + 1):
            for color, (grid, bias, root) in enumerate(((red, bias_r, root_r), (black, bias_k, root_k))):
                solved = solved + reduce_weight(dofs_ref, spot, color, x, lanes) * root[x] * grid[x]
                size = size + bias[x] * bias[x]
            first = red[x] * root_r[x]
            second = black[x] * root_k[x]
            odd = (place + x) % 2
            response.append(jnp.stack(
                [jnp.where(odd == 0, first, second), jnp.where(odd == 0, second, first)], axis=1))
        pooled.append(solved)
        norms.append(size)
    pooled = jnp.stack(pooled).reshape((2 * M, lanes))
    norms = jnp.stack(norms).reshape((2 * M, lanes)) * (diag_shift * diag_shift)
    pairs = jnp.where(
        lax.broadcasted_iota(jnp.int32, (M, 2 * M), 1) // 2
        == lax.broadcasted_iota(jnp.int32, (M, 2 * M), 0), 1.0, 0.0)
    schur = exact_dot(pairs, pooled)
    norms = exact_dot(pairs, norms)
    response = jnp.stack(response).reshape((PATCH, lanes))
    coarse = response.astype(jnp.bfloat16)
    fine = (response - coarse.astype(jnp.float32)).astype(jnp.bfloat16)
    coarse, fine = coarse.T, fine.T
    if part_ref.shape[0] > patches:
        block_ref[...] = jnp.zeros(block_ref.shape, jnp.float32)
        part_ref[...] = jnp.zeros(part_ref.shape, jnp.float32)
    identity = jnp.where(
        lax.broadcasted_iota(jnp.int32, (M, M), 0) == lax.broadcasted_iota(jnp.int32, (M, M), 1), 1.0, 0.0)
    p0, p1, p2 = start_polynomial()
    scaled, scales, inverse = [], [], []
    for p in range(patches):
        mine = slice(p * M, (p + 1) * M)
        size = norms[:, mine]
        down = lax.rsqrt(jnp.sum(size, axis=1, keepdims=True))
        across = lax.rsqrt(jnp.sum(size, axis=0, keepdims=True))
        scales.append((down, across))
        scaled.append(schur[:, mine] * down * across)
    for s in scaled:
        inverse.append(p0 * identity + p1 * s + p2 * exact_dot(s, s))
    for _ in range(newton_steps):
        rest = [2.0 * identity - exact_dot(s, g) for s, g in zip(scaled, inverse)]
        inverse = [exact_dot(g, r) for g, r in zip(inverse, rest)]
    for p in range(patches):
        mine = slice(p * M, (p + 1) * M)
        rows = rows_ref[p]
        projected = (jnp.dot(coarse[mine], rows, preferred_element_type=jnp.float32)
                     + jnp.dot(fine[mine], rows, preferred_element_type=jnp.float32))
        down, across = scales[p]
        block = inverse[p] * down * across
        block_ref[slot_ref[p]] = block
        part_ref[slot_ref[p]] = exact_dot(block, projected)


def reduce_weight(dofs_ref, spot, color, x, lanes):
    block = dofs_ref[color, 2, x * HALF * BOX:(x + 1) * HALF * BOX]
    return jnp.dot(block, spot, preferred_element_type=jnp.float32).reshape((HALF, BOX, lanes))


def two_colors(values):
    patches = values.shape[0]
    cells = values.reshape(patches, BOX, HALF, 2, BOX)
    odd = (jnp.arange(BOX)[:, None, None] + jnp.arange(BOX)[None, None, :]) % 2
    first, second = cells[:, :, :, 0], cells[:, :, :, 1]
    both = jnp.stack([jnp.where(odd == 0, first, second), jnp.where(odd == 0, second, first)])
    return both.reshape(2, patches, PATCH // 2).transpose(0, 2, 1)


def coarse_parts(target_slot, slot_count, coefficient, live, weights, patch_rows):
    dofs = jnp.stack([two_colors(v.astype(jnp.bfloat16)) for v in (coefficient, live, weights)], axis=1)
    patches = patch_rows.shape[0]
    lanes = patches * M
    omega = jnp.array(relaxation(), jnp.float32)
    smem = pl.BlockSpec(memory_space=pltpu.SMEM)
    vmem = pl.BlockSpec(memory_space=pltpu.VMEM)
    grid = pltpu.VMEM((BOX, HALF, BOX, lanes), jnp.float32)
    return pl.pallas_call(
        patch_kernel,
        out_shape=(jax.ShapeDtypeStruct((slot_count, M, M), jnp.float32),
                   jax.ShapeDtypeStruct((slot_count, M, patch_rows.shape[-1]), jnp.float32)),
        in_specs=[smem, smem, vmem, vmem],
        out_specs=(vmem, vmem),
        scratch_shapes=[grid] * 8,
        compiler_params=pltpu.CompilerParams(vmem_limit_bytes=40 * 1024 * 1024),
        cost_estimate=pl.CostEstimate(flops=10**9, bytes_accessed=2**21, transcendentals=0),
        name="patches",
    )(target_slot, omega, dofs, patch_rows)


def extended_2(array, sides, width):
    for axis, dim in sides:
        size, length = (lax.axis_size(axis), array.shape[dim])
        up = [(i, (i + 1) % size) for i in range(size - 1)]
        down = [(j, i) for i, j in up]
        last = lax.slice_in_dim(array, length - width, length, axis=dim)
        first = lax.slice_in_dim(array, 0, width, axis=dim)
        before = lax.ppermute(last, axis, up)
        after = lax.ppermute(first, axis, down)
        array = jnp.concatenate([before, array, after], axis=dim)
    return array


def local(fine_rhs, coef_table, coef_ids, localization, patch_mask, measure_weights, owners):
    extended = extended_2(fine_rhs, (("gx", 0), ("gy", 1), ("gz", 2)), HW)
    patch_count = localization.shape[0]
    extent = extended.shape[:3]
    rows = []
    for p in range(patch_count):
        first = localization[p, 0]
        corner = (first // (extent[1] * extent[2]), first // extent[2] % extent[1], first % extent[2], 0)
        box = lax.dynamic_slice(extended, corner, (BOX, BOX, BOX, extended.shape[-1]))
        rows.append(box.reshape(PATCH, -1))
    patch_rows = jnp.stack(rows)
    table_hits = (
        coef_ids[:, :, None] == jnp.arange(coef_table.shape[0], dtype=jnp.int32)[None, None, :]
    )
    coefficient = jnp.sum(
        jnp.where(table_hits, coef_table.astype(jnp.float32)[None, None, :], 0.0), axis=-1
    )
    groups = lax.axis_size("gz")
    capacity = max(patch_count // 4, (patch_count + groups - 1) // groups)
    slot_count = groups * capacity
    same = owners[:, None] == owners[None, :]
    earlier = jnp.arange(patch_count)[:, None] > jnp.arange(patch_count)[None, :]
    slot_rank = jnp.sum(jnp.where(same & earlier, 1, 0), axis=1).astype(jnp.int32)
    target_slot = owners * capacity + slot_rank
    blocks, parts = coarse_parts(target_slot, slot_count, coefficient, patch_mask, measure_weights, patch_rows)
    blocks = lax.all_to_all(blocks, "gz", split_axis=0, concat_axis=0, tiled=True)
    parts = lax.all_to_all(parts, "gz", split_axis=0, concat_axis=0, tiled=True)
    return (blocks.reshape(slot_count, -1), parts.reshape(slot_count, -1))


def solution(mesh):
    axes = ("gx", "gy", "gz")
    each = P(axes, None)
    return jax.shard_map(
        local,
        mesh=mesh,
        in_specs=(P("gx", "gy", "gz", None), P(), each, each, each, each, P(axes)),
        out_specs=(each, each),
        check_vma=False,
    )
```

```python
import math
import jax
import jax.numpy as jnp
from jax import lax
from jax.experimental import pallas as pl
from jax.experimental.pallas import tpu as pltpu
from jax.sharding import PartitionSpec as P

BOX = 8
HW = 4
PATCH = 512
M = 64
HALF = BOX // 2

diag_shift = 6.5
radius = 6.0 * math.cos(math.pi / 9.0) / diag_shift
low, high = (1.0 - radius) * diag_shift, (1.0 + radius) * diag_shift
half_steps = 30
newton_steps = 4
highest = lax.Precision.HIGHEST


def relaxation():
    weights = [1.0, 2.0 / (2.0 - radius * radius)]
    while len(weights) < half_steps:
        weights.append(1.0 / (1.0 - radius * radius * weights[-1] / 4.0))
    return weights


def start_polynomial():
    a, b = 1.0 / high, 1.0 / low
    mid, half = (a + b) / 2.0, (b - a) / 2.0
    t = -mid / half
    top = 4.0 * t**3 - 3.0 * t
    c3 = 4.0 / half**3 / top
    c2 = -12.0 * mid / half**3 / top
    c1 = (12.0 * mid * mid / half**3 - 3.0 / half) / top
    return (-c1, -c2, -c3)


def exact_dot(a, b):
    return jnp.dot(a, b, precision=highest, preferred_element_type=jnp.float32)


def relax(new, old, bias, gate, weight, flip, place):
    for x in range(BOX):
        here = old[x]
        up = pltpu.roll(here, 1, 1)
        down = pltpu.roll(here, BOX - 1, 1)
        total = jnp.where(place == 0, 0.0, up) + jnp.where(place == BOX - 1, 0.0, down)
        zero = jnp.zeros_like(here[:1])
        before = jnp.concatenate([zero, here[:-1]], axis=0)
        after = jnp.concatenate([here[1:], zero], axis=0)
        odd = (place + (x + flip)) % 2
        total = total + here + jnp.where(odd == 0, before, after)
        if x > 0:
            total = total + old[x - 1]
        if x < BOX - 1:
            total = total + old[x + 1]
        current = new[x]
        new[x] = current + weight * (gate[x] * total + bias[x] - current)


def patch_kernel(slot_ref, omega_ref, dofs_ref, rows_ref, out_ref,
                 red, black, bias_r, bias_k, gate_r, gate_k, root_r, root_k):
    patches = rows_ref.shape[0]
    lanes = patches * M
    spot = jnp.where(
        lax.broadcasted_iota(jnp.int32, (patches, lanes), 1) // M
        == lax.broadcasted_iota(jnp.int32, (patches, lanes), 0), 1.0, 0.0).astype(jnp.bfloat16)
    shape = (HALF, BOX, lanes)
    place = lax.broadcasted_iota(jnp.int32, shape, 1)
    column = lax.broadcasted_iota(jnp.int32, shape, 2) % M
    along = lax.broadcasted_iota(jnp.int32, shape, 0)
    for color, (bias, gate, root) in enumerate(((bias_r, gate_r, root_r), (bias_k, gate_k, root_k))):
        wide = [
            jnp.dot(dofs_ref[color, kind], spot, preferred_element_type=jnp.float32).reshape(
                (BOX, HALF, BOX, lanes))
            for kind in range(3)
        ]
        for x in range(BOX):
            live = wide[1][x]
            scale = live * lax.rsqrt(wide[0][x])
            member = (x // 2 * HALF + along) * HALF + place // 2 == column
            root[x] = scale
            gate[x] = live * (1.0 / diag_shift)
            bias[x] = jnp.where(member, scale * wide[2][x] * (1.0 / diag_shift), 0.0)
    red[...] = bias_r[...]
    black[...] = jnp.zeros(black.shape, jnp.float32)
    relax(black, red, bias_k, gate_k, omega_ref[1], 1, place)

    @pl.loop(1, half_steps // 2)
    def _(step):
        relax(red, black, bias_r, gate_r, omega_ref[2 * step], 0, place)
        relax(black, red, bias_k, gate_k, omega_ref[2 * step + 1], 1, place)

    pooled, norms, response = [], [], []
    for x2 in range(BOX // 2):
        solved, size = 0.0, 0.0
        for x in (2 * x2, 2 * x2 + 1):
            for color, (grid, bias, root) in enumerate(((red, bias_r, root_r), (black, bias_k, root_k))):
                solved = solved + reduce_weight(dofs_ref, spot, color, x, lanes) * root[x] * grid[x]
                size = size + bias[x] * bias[x]
            first = red[x] * root_r[x]
            second = black[x] * root_k[x]
            odd = (place + x) % 2
            response.append(jnp.stack(
                [jnp.where(odd == 0, first, second), jnp.where(odd == 0, second, first)], axis=1))
        pooled.append(solved)
        norms.append(size)
    pooled = jnp.stack(pooled).reshape((2 * M, lanes))
    norms = jnp.stack(norms).reshape((2 * M, lanes)) * (diag_shift * diag_shift)
    pairs = jnp.where(
        lax.broadcasted_iota(jnp.int32, (M, 2 * M), 1) // 2
        == lax.broadcasted_iota(jnp.int32, (M, 2 * M), 0), 1.0, 0.0)
    schur = exact_dot(pairs, pooled)
    norms = exact_dot(pairs, norms)
    response = jnp.stack(response).reshape((PATCH, lanes))
    coarse = response.astype(jnp.bfloat16)
    fine = (response - coarse.astype(jnp.float32)).astype(jnp.bfloat16)
    coarse, fine = coarse.T, fine.T
    width = rows_ref.shape[-1]
    if out_ref.shape[0] > patches:
        out_ref[...] = jnp.zeros(out_ref.shape, jnp.float32)
    identity = jnp.where(
        lax.broadcasted_iota(jnp.int32, (M, M), 0) == lax.broadcasted_iota(jnp.int32, (M, M), 1), 1.0, 0.0)
    p0, p1, p2 = start_polynomial()
    scaled, scales, inverse = [], [], []
    for p in range(patches):
        mine = slice(p * M, (p + 1) * M)
        size = norms[:, mine]
        down = lax.rsqrt(jnp.sum(size, axis=1, keepdims=True))
        across = lax.rsqrt(jnp.sum(size, axis=0, keepdims=True))
        scales.append((down, across))
        scaled.append(schur[:, mine] * down * across)
    for s in scaled:
        inverse.append(p0 * identity + p1 * s + p2 * exact_dot(s, s))
    for _ in range(newton_steps):
        rest = [2.0 * identity - exact_dot(s, g) for s, g in zip(scaled, inverse)]
        inverse = [exact_dot(g, r) for g, r in zip(inverse, rest)]
    for p in range(patches):
        mine = slice(p * M, (p + 1) * M)
        rows = rows_ref[p]
        projected = (jnp.dot(coarse[mine], rows, preferred_element_type=jnp.float32)
                     + jnp.dot(fine[mine], rows, preferred_element_type=jnp.float32))
        down, across = scales[p]
        block = inverse[p] * down * across
        out_ref[slot_ref[p], :, width:] = block
        out_ref[slot_ref[p], :, :width] = exact_dot(block, projected)


def reduce_weight(dofs_ref, spot, color, x, lanes):
    block = dofs_ref[color, 2, x * HALF * BOX:(x + 1) * HALF * BOX]
    return jnp.dot(block, spot, preferred_element_type=jnp.float32).reshape((HALF, BOX, lanes))


def two_colors(values):
    patches = values.shape[0]
    cells = values.reshape(patches, BOX, HALF, 2, BOX)
    odd = (jnp.arange(BOX)[:, None, None] + jnp.arange(BOX)[None, None, :]) % 2
    first, second = cells[:, :, :, 0], cells[:, :, :, 1]
    both = jnp.stack([jnp.where(odd == 0, first, second), jnp.where(odd == 0, second, first)])
    return both.reshape(2, patches, PATCH // 2).transpose(0, 2, 1)


def coarse_parts(target_slot, slot_count, coefficient, live, weights, patch_rows):
    dofs = jnp.stack([two_colors(v.astype(jnp.bfloat16)) for v in (coefficient, live, weights)], axis=1)
    patches = patch_rows.shape[0]
    lanes = patches * M
    omega = jnp.array(relaxation(), jnp.float32)
    smem = pl.BlockSpec(memory_space=pltpu.SMEM)
    vmem = pl.BlockSpec(memory_space=pltpu.VMEM)
    grid = pltpu.VMEM((BOX, HALF, BOX, lanes), jnp.float32)
    return pl.pallas_call(
        patch_kernel,
        out_shape=jax.ShapeDtypeStruct((slot_count, M, patch_rows.shape[-1] + M), jnp.float32),
        in_specs=[smem, smem, vmem, vmem],
        out_specs=vmem,
        scratch_shapes=[grid] * 8,
        compiler_params=pltpu.CompilerParams(vmem_limit_bytes=40 * 1024 * 1024),
        cost_estimate=pl.CostEstimate(flops=10**9, bytes_accessed=2**21, transcendentals=0),
        name="patches",
    )(target_slot, omega, dofs, patch_rows)


def up_down(axis):
    size = lax.axis_size(axis)
    up = [(i, i + 1) for i in range(size - 1)]
    return up, [(j, i) for i, j in up]


def edges(array, dim):
    length = array.shape[dim]
    return lax.slice_in_dim(array, length - HW, length, axis=dim), lax.slice_in_dim(array, 0, HW, axis=dim)


def exchanged(last, first, axis):
    up, down = up_down(axis)
    return lax.ppermute(last, axis, up), lax.ppermute(first, axis, down)


def widened(array, before, after, dim):
    pad = [(HW, HW, 0) if d == dim else (0, 0, 0) for d in range(array.ndim)]
    wide = lax.pad(array, jnp.zeros((), array.dtype), pad)
    wide = lax.dynamic_update_slice_in_dim(wide, before, 0, axis=dim)
    return lax.dynamic_update_slice_in_dim(wide, after, array.shape[dim] + HW, axis=dim)


def boxes(fine_rhs, localization):
    extent = [n + 2 * HW for n in fine_rhs.shape[:3]]
    corner = localization[:, 0]
    lower, upper = exchanged(corner, corner, "gz")
    before, after = exchanged(*edges(fine_rhs, 0), "gx")
    y_last, y_first = edges(fine_rhs, 1)
    last_y = jnp.concatenate([edges(before, 1)[0], y_last, edges(after, 1)[0]], axis=0)
    first_y = jnp.concatenate([edges(before, 1)[1], y_first, edges(after, 1)[1]], axis=0)
    y_before, y_after = exchanged(last_y, first_y, "gy")
    wide = widened(widened(fine_rhs, before, after, 0), y_before, y_after, 1)

    def window(source, first):
        at = (first // (extent[1] * extent[2]), first // extent[2] % extent[1], 0, 0)
        return lax.dynamic_slice(source, at, (BOX, BOX) + source.shape[2:])

    count = localization.shape[0]
    rising = [p for p in range(count) if p != 1]
    falling = [p for p in range(count) if p != 0]
    z_last, z_first = edges(wide, 2)
    sent_up = jnp.stack([window(z_last, upper[p]) for p in rising])
    sent_down = jnp.stack([window(z_first, lower[p]) for p in falling])
    z_before, z_after = exchanged(sent_up, sent_down, "gz")
    nothing = jnp.zeros((BOX, BOX, HW, fine_rhs.shape[-1]), fine_rhs.dtype)
    rows = []
    for p in range(count):
        low = z_before[rising.index(p)] if p in rising else nothing
        top = z_after[falling.index(p)] if p in falling else nothing
        column = jnp.concatenate([low, window(wide, corner[p]), top], axis=2)
        box = lax.dynamic_slice_in_dim(column, corner[p] % extent[2], BOX, axis=2)
        rows.append(box.reshape(PATCH, -1))
    return jnp.stack(rows)


def local(fine_rhs, coef_table, coef_ids, localization, patch_mask, measure_weights, owners):
    patch_count = localization.shape[0]
    patch_rows = boxes(fine_rhs, localization)
    table_hits = (
        coef_ids[:, :, None] == jnp.arange(coef_table.shape[0], dtype=jnp.int32)[None, None, :]
    )
    coefficient = jnp.sum(
        jnp.where(table_hits, coef_table.astype(jnp.float32)[None, None, :], 0.0), axis=-1
    )
    groups = lax.axis_size("gz")
    capacity = max(patch_count // 4, (patch_count + groups - 1) // groups)
    slot_count = groups * capacity
    same = owners[:, None] == owners[None, :]
    earlier = jnp.arange(patch_count)[:, None] > jnp.arange(patch_count)[None, :]
    slot_rank = jnp.sum(jnp.where(same & earlier, 1, 0), axis=1).astype(jnp.int32)
    target_slot = owners * capacity + slot_rank
    results = coarse_parts(target_slot, slot_count, coefficient, patch_mask, measure_weights, patch_rows)
    results = lax.all_to_all(results, "gz", split_axis=0, concat_axis=0, tiled=True)
    width = fine_rhs.shape[-1]
    return (results[:, :, width:].reshape(slot_count, -1), results[:, :, :width].reshape(slot_count, -1))


def solution(mesh):
    axes = ("gx", "gy", "gz")
    each = P(axes, None)
    return jax.shard_map(
        local,
        mesh=mesh,
        in_specs=(P("gx", "gy", "gz", None), P(), each, each, each, each, P(axes)),
        out_specs=(each, each),
        check_vma=False,
    )
```

```python
import math
import jax
import jax.numpy as jnp
from jax import lax
from jax.experimental import pallas as pl
from jax.experimental.pallas import tpu as pltpu
from jax.sharding import PartitionSpec as P

BOX = 8
HW = 4
PATCH = 512
M = 64
HALF = BOX // 2

diag_shift = 6.5
radius = 6.0 * math.cos(math.pi / 9.0) / diag_shift
low, high = (1.0 - radius) * diag_shift, (1.0 + radius) * diag_shift
half_steps = 30
newton_steps = 4
highest = lax.Precision.HIGHEST


def relaxation():
    weights = [1.0, 2.0 / (2.0 - radius * radius)]
    while len(weights) < half_steps:
        weights.append(1.0 / (1.0 - radius * radius * weights[-1] / 4.0))
    return weights


def start_polynomial():
    a, b = 1.0 / high, 1.0 / low
    mid, half = (a + b) / 2.0, (b - a) / 2.0
    t = -mid / half
    top = 4.0 * t**3 - 3.0 * t
    c3 = 4.0 / half**3 / top
    c2 = -12.0 * mid / half**3 / top
    c1 = (12.0 * mid * mid / half**3 - 3.0 / half) / top
    return (-c1, -c2, -c3)


def exact_dot(a, b):
    return jnp.dot(a, b, precision=highest, preferred_element_type=jnp.float32)


def relax(new, old, bias, gate, weight, flip, place):
    for x in range(BOX):
        here = old[x]
        up = pltpu.roll(here, 1, 1)
        down = pltpu.roll(here, BOX - 1, 1)
        total = jnp.where(place == 0, 0.0, up) + jnp.where(place == BOX - 1, 0.0, down)
        zero = jnp.zeros_like(here[:1])
        before = jnp.concatenate([zero, here[:-1]], axis=0)
        after = jnp.concatenate([here[1:], zero], axis=0)
        odd = (place + (x + flip)) % 2
        total = total + here + jnp.where(odd == 0, before, after)
        if x > 0:
            total = total + old[x - 1]
        if x < BOX - 1:
            total = total + old[x + 1]
        current = new[x]
        new[x] = current + weight * (gate[x] * total + bias[x] - current)


def patch_kernel(slot_ref, omega_ref, dofs_ref, rows_ref, out_ref,
                 red, black, bias_r, bias_k, gate_r, gate_k, root_r, root_k, load_r, load_k):
    patches = rows_ref.shape[0]
    lanes = patches * M
    cells = dofs_ref[...].T.astype(jnp.bfloat16)
    kinds = cells.shape[1]
    owner = lax.broadcasted_iota(jnp.int32, (kinds, lanes), 1) // M
    entry = lax.broadcasted_iota(jnp.int32, (kinds, lanes), 0)
    shape = (HALF, BOX, lanes)
    place = lax.broadcasted_iota(jnp.int32, shape, 1)
    column = lax.broadcasted_iota(jnp.int32, shape, 2) % M
    along = lax.broadcasted_iota(jnp.int32, shape, 0)
    wide = []
    for kind in range(3):
        spot = jnp.where(entry == kind * patches + owner, 1.0, 0.0).astype(jnp.bfloat16)
        wide.append(jnp.dot(cells, spot, preferred_element_type=jnp.float32).reshape(
            (BOX, HALF, 2, BOX, lanes)))
    for x in range(BOX):
        even = (place + x) % 2 == 0
        member = (x // 2 * HALF + along) * HALF + place // 2 == column
        pairs = [(w[x, :, 0], w[x, :, 1]) for w in wide]
        for bias, gate, root, load, swap in (
                (bias_r, gate_r, root_r, load_r, False), (bias_k, gate_k, root_k, load_k, True)):
            coef, live, weight = [
                jnp.where(even, b, a) if swap else jnp.where(even, a, b) for a, b in pairs]
            scale = live * lax.rsqrt(coef)
            root[x] = scale
            gate[x] = live * (1.0 / diag_shift)
            load[x] = scale * weight
            bias[x] = jnp.where(member, scale * weight * (1.0 / diag_shift), 0.0)
    red[...] = bias_r[...]
    black[...] = jnp.zeros(black.shape, jnp.float32)
    relax(black, red, bias_k, gate_k, omega_ref[1], 1, place)

    @pl.loop(1, half_steps // 2)
    def _(step):
        relax(red, black, bias_r, gate_r, omega_ref[2 * step], 0, place)
        relax(black, red, bias_k, gate_k, omega_ref[2 * step + 1], 1, place)

    pooled, norms, response = [], [], []
    for x2 in range(BOX // 2):
        solved, size = 0.0, 0.0
        for x in (2 * x2, 2 * x2 + 1):
            for grid, bias, load in ((red, bias_r, load_r), (black, bias_k, load_k)):
                solved = solved + load[x] * grid[x]
                size = size + bias[x] * bias[x]
            first = red[x] * root_r[x]
            second = black[x] * root_k[x]
            odd = (place + x) % 2
            response.append(jnp.stack(
                [jnp.where(odd == 0, first, second), jnp.where(odd == 0, second, first)], axis=1))
        pooled.append(solved)
        norms.append(size)
    pooled = jnp.stack(pooled).reshape((2 * M, lanes))
    norms = jnp.stack(norms).reshape((2 * M, lanes)) * (diag_shift * diag_shift)
    pairs = jnp.where(
        lax.broadcasted_iota(jnp.int32, (M, 2 * M), 1) // 2
        == lax.broadcasted_iota(jnp.int32, (M, 2 * M), 0), 1.0, 0.0)
    schur = exact_dot(pairs, pooled)
    norms = exact_dot(pairs, norms)
    response = jnp.stack(response).reshape((PATCH, lanes))
    coarse = response.astype(jnp.bfloat16)
    fine = (response - coarse.astype(jnp.float32)).astype(jnp.bfloat16)
    coarse, fine = coarse.T, fine.T
    width = rows_ref.shape[-1]
    if out_ref.shape[0] > patches:
        out_ref[...] = jnp.zeros(out_ref.shape, jnp.float32)
    identity = jnp.where(
        lax.broadcasted_iota(jnp.int32, (M, M), 0) == lax.broadcasted_iota(jnp.int32, (M, M), 1), 1.0, 0.0)
    p0, p1, p2 = start_polynomial()
    scaled, scales, inverse = [], [], []
    for p in range(patches):
        mine = slice(p * M, (p + 1) * M)
        size = norms[:, mine]
        down = lax.rsqrt(jnp.sum(size, axis=1, keepdims=True))
        across = lax.rsqrt(jnp.sum(size, axis=0, keepdims=True))
        scales.append((down, across))
        scaled.append(schur[:, mine] * down * across)
    for s in scaled:
        inverse.append(p0 * identity + p1 * s + p2 * exact_dot(s, s))
    for _ in range(newton_steps):
        rest = [2.0 * identity - exact_dot(s, g) for s, g in zip(scaled, inverse)]
        inverse = [exact_dot(g, r) for g, r in zip(inverse, rest)]
    for p in range(patches):
        mine = slice(p * M, (p + 1) * M)
        rows = rows_ref[p]
        projected = (jnp.dot(coarse[mine], rows, preferred_element_type=jnp.float32)
                     + jnp.dot(fine[mine], rows, preferred_element_type=jnp.float32))
        down, across = scales[p]
        block = inverse[p] * down * across
        out_ref[slot_ref[p], :, width:] = block
        out_ref[slot_ref[p], :, :width] = exact_dot(block, projected)


def coarse_parts(target_slot, slot_count, coefficient, live, weights, patch_rows):
    dofs = jnp.concatenate([v.astype(jnp.float32) for v in (coefficient, live, weights)], axis=0)
    dofs = jnp.pad(dofs, ((0, -dofs.shape[0] % 16), (0, 0)))
    patches = patch_rows.shape[0]
    lanes = patches * M
    omega = jnp.array(relaxation(), jnp.float32)
    smem = pl.BlockSpec(memory_space=pltpu.SMEM)
    vmem = pl.BlockSpec(memory_space=pltpu.VMEM)
    grid = pltpu.VMEM((BOX, HALF, BOX, lanes), jnp.float32)
    return pl.pallas_call(
        patch_kernel,
        out_shape=jax.ShapeDtypeStruct((slot_count, M, patch_rows.shape[-1] + M), jnp.float32),
        in_specs=[smem, smem, vmem, vmem],
        out_specs=vmem,
        scratch_shapes=[grid] * 10,
        compiler_params=pltpu.CompilerParams(vmem_limit_bytes=40 * 1024 * 1024),
        cost_estimate=pl.CostEstimate(flops=10**9, bytes_accessed=2**21, transcendentals=0),
        name="patches",
    )(target_slot, omega, dofs, patch_rows)


def up_down(axis):
    size = lax.axis_size(axis)
    up = [(i, i + 1) for i in range(size - 1)]
    return up, [(j, i) for i, j in up]


def edges(array, dim):
    length = array.shape[dim]
    return lax.slice_in_dim(array, length - HW, length, axis=dim), lax.slice_in_dim(array, 0, HW, axis=dim)


def exchanged(last, first, axis):
    up, down = up_down(axis)
    return lax.ppermute(last, axis, up), lax.ppermute(first, axis, down)


def widened(array, before, after, dim):
    pad = [(HW, HW, 0) if d == dim else (0, 0, 0) for d in range(array.ndim)]
    wide = lax.pad(array, jnp.zeros((), array.dtype), pad)
    wide = lax.dynamic_update_slice_in_dim(wide, before, 0, axis=dim)
    return lax.dynamic_update_slice_in_dim(wide, after, array.shape[dim] + HW, axis=dim)


def boxes(fine_rhs, localization):
    extent = [n + 2 * HW for n in fine_rhs.shape[:3]]
    first = localization[:, 0]
    corner = jnp.stack([
        lax.div(first, extent[1] * extent[2]),
        lax.rem(lax.div(first, extent[2]), extent[1]),
        lax.rem(first, extent[2])])
    lower, upper = exchanged(corner, corner, "gz")
    before, after = exchanged(*edges(fine_rhs, 0), "gx")
    y_last, y_first = edges(fine_rhs, 1)
    last_y = jnp.concatenate([edges(before, 1)[0], y_last, edges(after, 1)[0]], axis=0)
    first_y = jnp.concatenate([edges(before, 1)[1], y_first, edges(after, 1)[1]], axis=0)
    y_before, y_after = exchanged(last_y, first_y, "gy")
    wide = widened(widened(fine_rhs, before, after, 0), y_before, y_after, 1)

    zero = jnp.int32(0)

    def window(source, at, p):
        return lax.dynamic_slice(
            source, (at[0, p], at[1, p], zero, zero), (BOX, BOX) + source.shape[2:],
            allow_negative_indices=False)

    count = localization.shape[0]
    rising = [p for p in range(count) if p != 1]
    falling = [p for p in range(count) if p != 0]
    z_last, z_first = edges(wide, 2)
    sent_up = jnp.stack([window(z_last, upper, p) for p in rising])
    sent_down = jnp.stack([window(z_first, lower, p) for p in falling])
    z_before, z_after = exchanged(sent_up, sent_down, "gz")
    nothing = jnp.zeros((BOX, BOX, HW, fine_rhs.shape[-1]), fine_rhs.dtype)
    rows = []
    for p in range(count):
        low = z_before[rising.index(p)] if p in rising else nothing
        top = z_after[falling.index(p)] if p in falling else nothing
        column = jnp.concatenate([low, window(wide, corner, p), top], axis=2)
        box = lax.dynamic_slice(
            column, (zero, zero, corner[2, p], zero), (BOX, BOX, BOX, column.shape[3]),
            allow_negative_indices=False)
        rows.append(box.reshape(PATCH, -1))
    return jnp.stack(rows)


def local(fine_rhs, coef_table, coef_ids, localization, patch_mask, measure_weights, owners):
    patch_count = localization.shape[0]
    patch_rows = boxes(fine_rhs, localization)
    table_hits = (
        coef_ids[:, :, None] == jnp.arange(coef_table.shape[0], dtype=jnp.int32)[None, None, :]
    )
    coefficient = jnp.sum(
        jnp.where(table_hits, coef_table.astype(jnp.float32)[None, None, :], 0.0), axis=-1
    )
    groups = lax.axis_size("gz")
    capacity = max(patch_count // 4, (patch_count + groups - 1) // groups)
    slot_count = groups * capacity
    same = owners[:, None] == owners[None, :]
    earlier = jnp.arange(patch_count)[:, None] > jnp.arange(patch_count)[None, :]
    slot_rank = jnp.sum(jnp.where(same & earlier, 1, 0), axis=1).astype(jnp.int32)
    target_slot = owners * capacity + slot_rank
    results = coarse_parts(target_slot, slot_count, coefficient, patch_mask, measure_weights, patch_rows)
    results = lax.all_to_all(results, "gz", split_axis=0, concat_axis=0, tiled=True)
    width = fine_rhs.shape[-1]
    return (results[:, :, width:].reshape(slot_count, -1), results[:, :, :width].reshape(slot_count, -1))


def solution(mesh):
    axes = ("gx", "gy", "gz")
    each = P(axes, None)
    return jax.shard_map(
        local,
        mesh=mesh,
        in_specs=(P("gx", "gy", "gz", None), P(), each, each, each, each, P(axes)),
        out_specs=(each, each),
        check_vma=False,
    )
```

```python
import math
import jax
import jax.numpy as jnp
from jax import lax
from jax.experimental import pallas as pl
from jax.experimental.pallas import tpu as pltpu
from jax.sharding import PartitionSpec as P

BOX = 8
HW = 4
PATCH = 512
M = 64
HALF = BOX // 2

diag_shift = 6.5
radius = 6.0 * math.cos(math.pi / 9.0) / diag_shift
low, high = (1.0 - radius) * diag_shift, (1.0 + radius) * diag_shift
half_steps = 30
newton_steps = 4
highest = lax.Precision.HIGHEST


def relaxation():
    weights = [1.0, 2.0 / (2.0 - radius * radius)]
    while len(weights) < half_steps:
        weights.append(1.0 / (1.0 - radius * radius * weights[-1] / 4.0))
    return weights


def start_polynomial():
    a, b = 1.0 / high, 1.0 / low
    mid, half = (a + b) / 2.0, (b - a) / 2.0
    t = -mid / half
    top = 4.0 * t**3 - 3.0 * t
    c3 = 4.0 / half**3 / top
    c2 = -12.0 * mid / half**3 / top
    c1 = (12.0 * mid * mid / half**3 - 3.0 / half) / top
    return (-c1, -c2, -c3)


def exact_dot(a, b):
    return jnp.dot(a, b, precision=highest, preferred_element_type=jnp.float32)


def relax(new, old, bias, gate, weight, flip, place):
    for x in range(BOX):
        here = old[x]
        up = pltpu.roll(here, 1, 1)
        down = pltpu.roll(here, BOX - 1, 1)
        total = jnp.where(place == 0, 0.0, up) + jnp.where(place == BOX - 1, 0.0, down)
        zero = jnp.zeros_like(here[:1])
        before = jnp.concatenate([zero, here[:-1]], axis=0)
        after = jnp.concatenate([here[1:], zero], axis=0)
        odd = (place + (x + flip)) % 2
        total = total + here + jnp.where(odd == 0, before, after)
        if x > 0:
            total = total + old[x - 1]
        if x < BOX - 1:
            total = total + old[x + 1]
        current = new[x]
        new[x] = current + weight * (gate[x] * total + bias[x] - current)


def patch_kernel(slot_ref, omega_ref, dofs_ref, rows_ref, out_ref,
                 red, black, bias_r, bias_k, gate_r, gate_k, root_r, root_k, load_r, load_k):
    patches = rows_ref.shape[0]
    lanes = patches * M
    cells = dofs_ref[...].T.astype(jnp.bfloat16)
    kinds = cells.shape[1]
    owner = lax.broadcasted_iota(jnp.int32, (kinds, lanes), 1) // M
    entry = lax.broadcasted_iota(jnp.int32, (kinds, lanes), 0)
    shape = (HALF, BOX, lanes)
    place = lax.broadcasted_iota(jnp.int32, shape, 1)
    column = lax.broadcasted_iota(jnp.int32, shape, 2) % M
    along = lax.broadcasted_iota(jnp.int32, shape, 0)
    wide = []
    for kind in range(3):
        spot = jnp.where(entry == kind * patches + owner, 1.0, 0.0).astype(jnp.bfloat16)
        wide.append(jnp.dot(cells, spot, preferred_element_type=jnp.float32).reshape(
            (BOX, HALF, 2, BOX, lanes)))
    for x in range(BOX):
        even = (place + x) % 2 == 0
        member = (x // 2 * HALF + along) * HALF + place // 2 == column
        pairs = [(w[x, :, 0], w[x, :, 1]) for w in wide]
        for bias, gate, root, load, swap in (
                (bias_r, gate_r, root_r, load_r, False), (bias_k, gate_k, root_k, load_k, True)):
            coef, live, weight = [
                jnp.where(even, b, a) if swap else jnp.where(even, a, b) for a, b in pairs]
            scale = live * lax.rsqrt(coef)
            root[x] = scale
            gate[x] = live * (1.0 / diag_shift)
            load[x] = scale * weight
            bias[x] = jnp.where(member, scale * weight * (1.0 / diag_shift), 0.0)
    red[...] = bias_r[...]
    black[...] = jnp.zeros(black.shape, jnp.float32)
    relax(black, red, bias_k, gate_k, omega_ref[1], 1, place)

    @pl.loop(1, half_steps // 2)
    def _(step):
        relax(red, black, bias_r, gate_r, omega_ref[2 * step], 0, place)
        relax(black, red, bias_k, gate_k, omega_ref[2 * step + 1], 1, place)

    pooled, norms, response = [], [], []
    for x2 in range(BOX // 2):
        solved, size = 0.0, 0.0
        for x in (2 * x2, 2 * x2 + 1):
            for grid, bias, load in ((red, bias_r, load_r), (black, bias_k, load_k)):
                solved = solved + load[x] * grid[x]
                size = size + bias[x] * bias[x]
            first = red[x] * root_r[x]
            second = black[x] * root_k[x]
            odd = (place + x) % 2
            response.append(jnp.stack(
                [jnp.where(odd == 0, first, second), jnp.where(odd == 0, second, first)], axis=1))
        pooled.append(solved)
        norms.append(size)
    pooled = jnp.stack(pooled).reshape((2 * M, lanes))
    norms = jnp.stack(norms).reshape((2 * M, lanes)) * (diag_shift * diag_shift)
    pairs = jnp.where(
        lax.broadcasted_iota(jnp.int32, (M, 2 * M), 1) // 2
        == lax.broadcasted_iota(jnp.int32, (M, 2 * M), 0), 1.0, 0.0)
    schur = exact_dot(pairs, pooled)
    norms = exact_dot(pairs, norms)
    response = jnp.stack(response).reshape((PATCH, lanes))
    coarse = response.astype(jnp.bfloat16)
    fine = (response - coarse.astype(jnp.float32)).astype(jnp.bfloat16)
    coarse, fine = coarse.T, fine.T
    width = rows_ref.shape[-1]
    if out_ref.shape[0] > patches:
        out_ref[...] = jnp.zeros(out_ref.shape, jnp.float32)
    identity = jnp.where(
        lax.broadcasted_iota(jnp.int32, (M, M), 0) == lax.broadcasted_iota(jnp.int32, (M, M), 1), 1.0, 0.0)
    p0, p1, p2 = start_polynomial()
    scaled, scales, inverse = [], [], []
    for p in range(patches):
        mine = slice(p * M, (p + 1) * M)
        size = norms[:, mine]
        down = lax.rsqrt(jnp.sum(size, axis=1, keepdims=True))
        across = lax.rsqrt(jnp.sum(size, axis=0, keepdims=True))
        scales.append((down, across))
        scaled.append(schur[:, mine] * down * across)
    for s in scaled:
        inverse.append(p0 * identity + p1 * s + p2 * exact_dot(s, s))
    for _ in range(newton_steps):
        rest = [2.0 * identity - exact_dot(s, g) for s, g in zip(scaled, inverse)]
        inverse = [exact_dot(g, r) for g, r in zip(inverse, rest)]
    for p in range(patches):
        mine = slice(p * M, (p + 1) * M)
        rows = rows_ref[p]
        projected = (jnp.dot(coarse[mine], rows, preferred_element_type=jnp.float32)
                     + jnp.dot(fine[mine], rows, preferred_element_type=jnp.float32))
        down, across = scales[p]
        block = inverse[p] * down * across
        out_ref[slot_ref[p], :, width:] = block
        out_ref[slot_ref[p], :, :width] = exact_dot(block, projected)


def coarse_parts(target_slot, slot_count, coefficient, live, weights, patch_rows):
    dofs = jnp.concatenate([v.astype(jnp.float32) for v in (coefficient, live, weights)], axis=0)
    dofs = jnp.pad(dofs, ((0, -dofs.shape[0] % 16), (0, 0)))
    patches = patch_rows.shape[0]
    lanes = patches * M
    omega = jnp.array(relaxation(), jnp.float32)
    smem = pl.BlockSpec(memory_space=pltpu.SMEM)
    vmem = pl.BlockSpec(memory_space=pltpu.VMEM)
    grid = pltpu.VMEM((BOX, HALF, BOX, lanes), jnp.float32)
    return pl.pallas_call(
        patch_kernel,
        out_shape=jax.ShapeDtypeStruct((slot_count, M, patch_rows.shape[-1] + M), jnp.float32),
        in_specs=[smem, smem, vmem, vmem],
        out_specs=vmem,
        scratch_shapes=[grid] * 10,
        compiler_params=pltpu.CompilerParams(vmem_limit_bytes=40 * 1024 * 1024),
        cost_estimate=pl.CostEstimate(flops=10**9, bytes_accessed=2**21, transcendentals=0),
        name="patches",
    )(target_slot, omega, dofs, patch_rows)


def up_down(axis):
    size = lax.axis_size(axis)
    up = [(i, i + 1) for i in range(size - 1)]
    return up, [(j, i) for i, j in up]


def edges(array, dim):
    length = array.shape[dim]
    return lax.slice_in_dim(array, length - HW, length, axis=dim), lax.slice_in_dim(array, 0, HW, axis=dim)


def exchanged(last, first, axis):
    up, down = up_down(axis)
    return lax.ppermute(last, axis, up), lax.ppermute(first, axis, down)


def boxes(fine_rhs, localization):
    extent = [n + 2 * HW for n in fine_rhs.shape[:3]]
    first = localization[:, 0]
    corner = jnp.stack([
        lax.div(first, extent[1] * extent[2]),
        lax.rem(lax.div(first, extent[2]), extent[1]),
        lax.rem(first, extent[2])])
    lower, upper = exchanged(corner, corner, "gz")
    before, after = exchanged(*edges(fine_rhs, 0), "gx")
    y_last, y_first = edges(fine_rhs, 1)
    last_y = jnp.concatenate([edges(before, 1)[0], y_last, edges(after, 1)[0]], axis=0)
    first_y = jnp.concatenate([edges(before, 1)[1], y_first, edges(after, 1)[1]], axis=0)
    y_before, y_after = exchanged(last_y, first_y, "gy")
    side, none = (HW, HW, 0), (0, 0, 0)
    wide = lax.pad(fine_rhs, jnp.zeros((), fine_rhs.dtype), [side, side, none, none])
    for piece, at in ((before, (0, HW)), (after, (extent[0] - HW, HW)),
                      (y_before, (0, 0)), (y_after, (0, extent[1] - HW))):
        wide = lax.dynamic_update_slice(wide, piece, at + (0, 0))

    zero = jnp.int32(0)

    def window(source, at, p):
        return lax.dynamic_slice(
            source, (at[0, p], at[1, p], zero, zero), (BOX, BOX) + source.shape[2:],
            allow_negative_indices=False)

    count = localization.shape[0]
    rising = [p for p in range(count) if p != 1]
    falling = [p for p in range(count) if p != 0]
    z_last, z_first = edges(wide, 2)
    sent_up = jnp.stack([window(z_last, upper, p) for p in rising])
    sent_down = jnp.stack([window(z_first, lower, p) for p in falling])
    z_before, z_after = exchanged(sent_up, sent_down, "gz")
    nothing = jnp.zeros((BOX, BOX, HW, fine_rhs.shape[-1]), fine_rhs.dtype)
    rows = []
    for p in range(count):
        low = z_before[rising.index(p)] if p in rising else nothing
        top = z_after[falling.index(p)] if p in falling else nothing
        column = jnp.concatenate([low, window(wide, corner, p), top], axis=2)
        box = lax.dynamic_slice(
            column, (zero, zero, corner[2, p], zero), (BOX, BOX, BOX, column.shape[3]),
            allow_negative_indices=False)
        rows.append(box.reshape(PATCH, -1))
    return jnp.stack(rows)


def local(fine_rhs, coef_table, coef_ids, localization, patch_mask, measure_weights, owners):
    patch_count = localization.shape[0]
    patch_rows = boxes(fine_rhs, localization)
    table_hits = (
        coef_ids[:, :, None] == jnp.arange(coef_table.shape[0], dtype=jnp.int32)[None, None, :]
    )
    coefficient = jnp.sum(
        jnp.where(table_hits, coef_table.astype(jnp.float32)[None, None, :], 0.0), axis=-1
    )
    groups = lax.axis_size("gz")
    capacity = max(patch_count // 4, (patch_count + groups - 1) // groups)
    slot_count = groups * capacity
    same = owners[:, None] == owners[None, :]
    earlier = jnp.arange(patch_count)[:, None] > jnp.arange(patch_count)[None, :]
    slot_rank = jnp.sum(jnp.where(same & earlier, 1, 0), axis=1).astype(jnp.int32)
    target_slot = owners * capacity + slot_rank
    results = coarse_parts(target_slot, slot_count, coefficient, patch_mask, measure_weights, patch_rows)
    results = lax.all_to_all(results, "gz", split_axis=0, concat_axis=0, tiled=True)
    width = fine_rhs.shape[-1]
    return (results[:, :, width:].reshape(slot_count, -1), results[:, :, :width].reshape(slot_count, -1))


def solution(mesh):
    axes = ("gx", "gy", "gz")
    each = P(axes, None)
    return jax.shard_map(
        local,
        mesh=mesh,
        in_specs=(P("gx", "gy", "gz", None), P(), each, each, each, each, P(axes)),
        out_specs=(each, each),
        check_vma=False,
    )
```

```python
import math
import jax
import jax.numpy as jnp
from jax import lax
from jax.experimental import pallas as pl
from jax.experimental.pallas import tpu as pltpu
from jax.sharding import PartitionSpec as P

BOX = 8
HW = 4
PATCH = 512
M = 64
HALF = BOX // 2

diag_shift = 6.5
radius = 6.0 * math.cos(math.pi / 9.0) / diag_shift
low, high = (1.0 - radius) * diag_shift, (1.0 + radius) * diag_shift
half_steps = 30
newton_steps = 4
highest = lax.Precision.HIGHEST


def relaxation():
    weights = [1.0, 2.0 / (2.0 - radius * radius)]
    while len(weights) < half_steps:
        weights.append(1.0 / (1.0 - radius * radius * weights[-1] / 4.0))
    return weights


def start_polynomial():
    a, b = 1.0 / high, 1.0 / low
    mid, half = (a + b) / 2.0, (b - a) / 2.0
    t = -mid / half
    top = 4.0 * t**3 - 3.0 * t
    c3 = 4.0 / half**3 / top
    c2 = -12.0 * mid / half**3 / top
    c1 = (12.0 * mid * mid / half**3 - 3.0 / half) / top
    return (-c1, -c2, -c3)


def exact_dot(a, b):
    return jnp.dot(a, b, precision=highest, preferred_element_type=jnp.float32)


def relax(new, old, bias, gate, weight, flip, place):
    for x in range(BOX):
        here = old[x]
        up = pltpu.roll(here, 1, 1)
        down = pltpu.roll(here, BOX - 1, 1)
        total = jnp.where(place == 0, 0.0, up) + jnp.where(place == BOX - 1, 0.0, down)
        zero = jnp.zeros_like(here[:1])
        before = jnp.concatenate([zero, here[:-1]], axis=0)
        after = jnp.concatenate([here[1:], zero], axis=0)
        odd = (place + (x + flip)) % 2
        total = total + here + jnp.where(odd == 0, before, after)
        if x > 0:
            total = total + old[x - 1]
        if x < BOX - 1:
            total = total + old[x + 1]
        current = new[x]
        new[x] = current + weight * (gate[x] * total + bias[x] - current)


def patch_kernel(slot_ref, omega_ref, dofs_ref, rows_ref, out_ref,
                 red, black, bias_r, bias_k, gate_r, gate_k, root_r, root_k, load_r, load_k):
    patches = rows_ref.shape[0]
    lanes = patches * M
    cells = dofs_ref[...].T.astype(jnp.bfloat16)
    kinds = cells.shape[1]
    owner = lax.broadcasted_iota(jnp.int32, (kinds, lanes), 1) // M
    entry = lax.broadcasted_iota(jnp.int32, (kinds, lanes), 0)
    shape = (HALF, BOX, lanes)
    place = lax.broadcasted_iota(jnp.int32, shape, 1)
    column = lax.broadcasted_iota(jnp.int32, shape, 2) % M
    along = lax.broadcasted_iota(jnp.int32, shape, 0)
    wide = []
    for kind in range(3):
        spot = jnp.where(entry == kind * patches + owner, 1.0, 0.0).astype(jnp.bfloat16)
        wide.append(jnp.dot(cells, spot, preferred_element_type=jnp.float32).reshape(
            (BOX, HALF, 2, BOX, lanes)))
    for x in range(BOX):
        even = (place + x) % 2 == 0
        member = (x // 2 * HALF + along) * HALF + place // 2 == column
        pairs = [(w[x, :, 0], w[x, :, 1]) for w in wide]
        for bias, gate, root, load, swap in (
                (bias_r, gate_r, root_r, load_r, False), (bias_k, gate_k, root_k, load_k, True)):
            coef, live, weight = [
                jnp.where(even, b, a) if swap else jnp.where(even, a, b) for a, b in pairs]
            scale = live * lax.rsqrt(coef)
            root[x] = scale
            gate[x] = live * (1.0 / diag_shift)
            load[x] = scale * weight
            bias[x] = jnp.where(member, scale * weight * (1.0 / diag_shift), 0.0)
    red[...] = bias_r[...]
    black[...] = jnp.zeros(black.shape, jnp.float32)
    relax(black, red, bias_k, gate_k, omega_ref[1], 1, place)

    @pl.loop(1, half_steps // 2)
    def _(step):
        relax(red, black, bias_r, gate_r, omega_ref[2 * step], 0, place)
        relax(black, red, bias_k, gate_k, omega_ref[2 * step + 1], 1, place)

    pooled, norms, response = [], [], []
    for x2 in range(BOX // 2):
        solved, size = 0.0, 0.0
        for x in (2 * x2, 2 * x2 + 1):
            for grid, bias, load in ((red, bias_r, load_r), (black, bias_k, load_k)):
                solved = solved + load[x] * grid[x]
                size = size + bias[x] * bias[x]
            first = red[x] * root_r[x]
            second = black[x] * root_k[x]
            odd = (place + x) % 2
            response.append(jnp.stack(
                [jnp.where(odd == 0, first, second), jnp.where(odd == 0, second, first)], axis=1))
        pooled.append(solved)
        norms.append(size)
    pooled = jnp.stack(pooled).reshape((2 * M, lanes))
    norms = jnp.stack(norms).reshape((2 * M, lanes)) * (diag_shift * diag_shift)
    pairs = jnp.where(
        lax.broadcasted_iota(jnp.int32, (M, 2 * M), 1) // 2
        == lax.broadcasted_iota(jnp.int32, (M, 2 * M), 0), 1.0, 0.0)
    schur = exact_dot(pairs, pooled)
    norms = exact_dot(pairs, norms)
    response = jnp.stack(response).reshape((PATCH, lanes))
    coarse = response.astype(jnp.bfloat16)
    fine = (response - coarse.astype(jnp.float32)).astype(jnp.bfloat16)
    coarse, fine = coarse.T, fine.T
    width = rows_ref.shape[-1]
    if out_ref.shape[0] > patches:
        out_ref[...] = jnp.zeros(out_ref.shape, jnp.float32)
    identity = jnp.where(
        lax.broadcasted_iota(jnp.int32, (M, M), 0) == lax.broadcasted_iota(jnp.int32, (M, M), 1), 1.0, 0.0)
    p0, p1, p2 = start_polynomial()
    scaled, scales, inverse = [], [], []
    for p in range(patches):
        mine = slice(p * M, (p + 1) * M)
        size = norms[:, mine]
        down = lax.rsqrt(jnp.sum(size, axis=1, keepdims=True))
        across = lax.rsqrt(jnp.sum(size, axis=0, keepdims=True))
        scales.append((down, across))
        scaled.append(schur[:, mine] * down * across)
    for s in scaled:
        inverse.append(p0 * identity + p1 * s + p2 * exact_dot(s, s))
    for _ in range(newton_steps):
        rest = [2.0 * identity - exact_dot(s, g) for s, g in zip(scaled, inverse)]
        inverse = [exact_dot(g, r) for g, r in zip(inverse, rest)]
    for p in range(patches):
        mine = slice(p * M, (p + 1) * M)
        rows = rows_ref[p]
        projected = (jnp.dot(coarse[mine], rows, preferred_element_type=jnp.float32)
                     + jnp.dot(fine[mine], rows, preferred_element_type=jnp.float32))
        down, across = scales[p]
        block = inverse[p] * down * across
        out_ref[slot_ref[p], :, width:] = block
        out_ref[slot_ref[p], :, :width] = exact_dot(block, projected)


def coarse_parts(target_slot, slot_count, coefficient, live, weights, patch_rows):
    dofs = jnp.concatenate([v.astype(jnp.float32) for v in (coefficient, live, weights)], axis=0)
    dofs = jnp.pad(dofs, ((0, -dofs.shape[0] % 16), (0, 0)))
    patches = patch_rows.shape[0]
    lanes = patches * M
    omega = jnp.array(relaxation(), jnp.float32)
    smem = pl.BlockSpec(memory_space=pltpu.SMEM)
    vmem = pl.BlockSpec(memory_space=pltpu.VMEM)
    grid = pltpu.VMEM((BOX, HALF, BOX, lanes), jnp.float32)
    return pl.pallas_call(
        patch_kernel,
        out_shape=jax.ShapeDtypeStruct((slot_count, M, patch_rows.shape[-1] + M), jnp.float32),
        in_specs=[smem, smem, vmem, vmem],
        out_specs=vmem,
        scratch_shapes=[grid] * 10,
        compiler_params=pltpu.CompilerParams(vmem_limit_bytes=40 * 1024 * 1024),
        cost_estimate=pl.CostEstimate(flops=10**9, bytes_accessed=2**21, transcendentals=0),
        name="patches",
    )(target_slot, omega, dofs, patch_rows)


def up_down(axis):
    size = lax.axis_size(axis)
    up = [(i, i + 1) for i in range(size - 1)]
    return up, [(j, i) for i, j in up]


def edges(array, dim):
    length = array.shape[dim]
    return lax.slice_in_dim(array, length - HW, length, axis=dim), lax.slice_in_dim(array, 0, HW, axis=dim)


def exchanged(last, first, axis):
    up, down = up_down(axis)
    return lax.ppermute(last, axis, up), lax.ppermute(first, axis, down)


def boxes(fine_rhs, localization):
    extent = [n + 2 * HW for n in fine_rhs.shape[:3]]
    first = localization[:, 0]
    corner = jnp.stack([
        lax.div(first, extent[1] * extent[2]),
        lax.rem(lax.div(first, extent[2]), extent[1]),
        lax.rem(first, extent[2])])
    lower, upper = exchanged(corner, corner, "gz")
    before, after = exchanged(*edges(fine_rhs, 0), "gx")
    y_last, y_first = edges(fine_rhs, 1)
    last_y = jnp.concatenate([edges(before, 1)[0], y_last, edges(after, 1)[0]], axis=0)
    first_y = jnp.concatenate([edges(before, 1)[1], y_first, edges(after, 1)[1]], axis=0)
    y_before, y_after = exchanged(last_y, first_y, "gy")
    side, none = (HW, HW, 0), (0, 0, 0)
    wide = lax.pad(fine_rhs, jnp.zeros((), fine_rhs.dtype), [side, side, none, none])
    for piece, at in ((before, (0, HW)), (after, (extent[0] - HW, HW)),
                      (y_before, (0, 0)), (y_after, (0, extent[1] - HW))):
        wide = lax.dynamic_update_slice(wide, piece, at + (0, 0))

    zero = jnp.int32(0)

    def window(source, at, p):
        return lax.dynamic_slice(
            source, (at[0, p], at[1, p], zero, zero), (BOX, BOX) + source.shape[2:],
            allow_negative_indices=False)

    count = localization.shape[0]
    rising = [p for p in range(count) if p != 1]
    falling = [p for p in range(count) if p != 0]
    sent_up = jnp.stack([edges(window(wide, upper, p), 2)[0] for p in rising])
    sent_down = jnp.stack([edges(window(wide, lower, p), 2)[1] for p in falling])
    z_before, z_after = exchanged(sent_up, sent_down, "gz")
    nothing = jnp.zeros((BOX, BOX, HW, fine_rhs.shape[-1]), fine_rhs.dtype)
    rows = []
    for p in range(count):
        low = z_before[rising.index(p)] if p in rising else nothing
        top = z_after[falling.index(p)] if p in falling else nothing
        column = jnp.concatenate([low, window(wide, corner, p), top], axis=2)
        box = lax.dynamic_slice(
            column, (zero, zero, corner[2, p], zero), (BOX, BOX, BOX, column.shape[3]),
            allow_negative_indices=False)
        rows.append(box.reshape(PATCH, -1))
    return jnp.stack(rows)


def local(fine_rhs, coef_table, coef_ids, localization, patch_mask, measure_weights, owners):
    patch_count = localization.shape[0]
    patch_rows = boxes(fine_rhs, localization)
    table_hits = (
        coef_ids[:, :, None] == jnp.arange(coef_table.shape[0], dtype=jnp.int32)[None, None, :]
    )
    coefficient = jnp.sum(
        jnp.where(table_hits, coef_table.astype(jnp.float32)[None, None, :], 0.0), axis=-1
    )
    groups = lax.axis_size("gz")
    capacity = max(patch_count // 4, (patch_count + groups - 1) // groups)
    slot_count = groups * capacity
    same = owners[:, None] == owners[None, :]
    earlier = jnp.arange(patch_count)[:, None] > jnp.arange(patch_count)[None, :]
    slot_rank = jnp.sum(jnp.where(same & earlier, 1, 0), axis=1).astype(jnp.int32)
    target_slot = owners * capacity + slot_rank
    results = coarse_parts(target_slot, slot_count, coefficient, patch_mask, measure_weights, patch_rows)
    results = lax.all_to_all(results, "gz", split_axis=0, concat_axis=0, tiled=True)
    width = fine_rhs.shape[-1]
    return (results[:, :, width:].reshape(slot_count, -1), results[:, :, :width].reshape(slot_count, -1))


def solution(mesh):
    axes = ("gx", "gy", "gz")
    each = P(axes, None)
    return jax.shard_map(
        local,
        mesh=mesh,
        in_specs=(P("gx", "gy", "gz", None), P(), each, each, each, each, P(axes)),
        out_specs=(each, each),
        check_vma=False,
    )
```
